32 devices in a mesh: dp: 8 (over z, x), feat: 4 (over y, core).
Axes of the slice: x: 2, y: 2, z: 4, core: 2. Of those that a mesh axis runs over, the one named last changes fastest.
Arguments:
- samples: bfloat16 [8192, 1024], P('dp', 'feat'), may hold values from -6 to 6
- freqs: bfloat16 [1024, 32768], P('dp', 'feat'), may hold values from -0.1875 to 0.1875
- phases: float32 [32768], P('feat'), may hold values from -3.140625 to 3.140625
- range_test: bfloat16 [32768, 256], P('feat'), may hold values from -6 to 6
- corange_test: bfloat16 [256, 8192], P(None, 'dp'), may hold values from -6 to 6
Outputs:
- range_sketch: float32 [8192, 256], P(('dp', 'feat'))
- corange_sketch: float32 [256, 32768], P('dp', 'feat')
The draws below stay inside these ranges and needn't reach their ends.
All inputs are finite; a program needn't handle non-finite values.
Results may differ from the reference program's by a relative error of at most 0.0024.
Values may be sent and summed in bfloat16 or wider, within the bound.
A program may use at most 128 MiB of HBM per device.

```python
import math
import jax
import jax.numpy as jnp
from jax import lax

E = 1024
F = 32768
K = 256
S_DEV = 1024
SAMPLES = 8192


def spiked(drawn, own_key, source, target, shards_of, factor):
    def block_of(dim):
        return (jnp.arange(drawn.shape[dim]) // (drawn.shape[dim] // shards_of)).reshape((-1,) + (1,) * (drawn.ndim - 1 - dim))

    first = jax.random.permutation(own_key, shards_of)[block_of(target)]
    far = (block_of(target) + shards_of // 2) % shards_of
    return jnp.where((block_of(source) == first) | (block_of(source) == far), factor * drawn, drawn)


def block_scale(stream_key, shape, pieces, smallest, high):
    gain = 1.0
    for dim, shards_of in pieces:
        draws = jax.random.uniform(jax.random.fold_in(jax.random.fold_in(stream_key, 6), dim), (shards_of,), jnp.float32, smallest / len(pieces), high / len(pieces))
        gain = gain * jnp.repeat(jnp.exp(draws), shape[dim] // shards_of).reshape((-1,) + (1,) * (len(shape) - 1 - dim))
    return gain


def scatter_about(stream_key, extent, spread, bound, cuts=(), kind=jnp.bfloat16):
    factor_of = block_scale(stream_key, extent, cuts, -0.22, 0.18) if cuts else 1.0
    values = jax.random.normal(stream_key, extent, jnp.float32) * spread * factor_of
    return jnp.minimum(jnp.maximum(values, -bound), bound).astype(kind)


def heavy_noise(own_key, extent, spread, most, split, heavy, kind=jnp.bfloat16):
    result = spread * jax.random.normal(own_key, extent, jnp.float32)
    if split:
        result = result * block_scale(own_key, extent, split, -0.22, 0.18)
    return jnp.clip(spiked(result, jax.random.fold_in(own_key, 3), *heavy), -most, most).astype(kind)


def setup_inputs(seed: int = 0) -> dict:
    key_list = jax.random.split(jax.random.key(seed), 6)
    return {
        "samples": scatter_about(key_list[0], (SAMPLES, E), 1.0, 6.0, ((0, 8), (1, 4))),
        "freqs": scatter_about(key_list[1], (E, F), E ** -0.5, 0.1875, ((0, 8), (1, 4))),
        "phases": jnp.clip(jax.random.uniform(key_list[2], (F,), jnp.float32, -3.140625, 3.140625), -3.140625, 3.140625),
        "range_test": scatter_about(key_list[3], (F, K), 1.0, 6.0, ((0, 4),)),
        "corange_test": heavy_noise(key_list[4], (K, SAMPLES), 1.0, 6.0, ((1, 8),), (1, 0, 8, 2.0)),
    }


def reference(samples, freqs, phases, range_test, corange_test):
    scale = math.sqrt(2.0 / F)
    blocks = SAMPLES // S_DEV
    sample_blocks = samples.reshape(blocks, S_DEV, E)
    test_blocks = corange_test.reshape(K, blocks, S_DEV).transpose(1, 0, 2)

    def one_block(carry, inputs):
        rows, tests = inputs
        projection = jnp.dot(rows, freqs, preferred_element_type=jnp.float32)
        features = (scale * jnp.cos(projection + phases[None, :])).astype(jnp.bfloat16)
        range_rows = jnp.dot(features, range_test, preferred_element_type=jnp.float32)
        carry = carry + jnp.dot(tests, features, preferred_element_type=jnp.float32)
        return (carry, range_rows)
    start = jnp.zeros((K, F), jnp.float32)
    corange_sketch, range_rows = lax.scan(one_block, start, (sample_blocks, test_blocks))
    return (range_rows.reshape(SAMPLES, K), corange_sketch)
```

```python
import functools
import math

import jax
import jax.numpy as jnp
from jax import lax
from jax.experimental import pallas as pl
from jax.experimental.pallas import tpu as pltpu
from jax.sharding import PartitionSpec as P

MESH = pl.DeviceIdType.MESH
INV_TURN = 1.0 / (2.0 * math.pi)
SIN_TURN = (6.283164044278293, -41.33714236799647, 81.34076878818043, -70.99343236149275)
WIRE = jnp.float32
LANES = 128


def scaled_cos(turns, scale):
    nearest = lax.round(turns, lax.RoundingMethod.TO_NEAREST_EVEN)
    g = 0.25 - jnp.abs(turns - nearest)
    s = g * g
    poly = jnp.float32(SIN_TURN[-1] * scale)
    for coef in SIN_TURN[-2::-1]:
        poly = poly * s + jnp.float32(coef * scale)
    return poly * g


def kernel(
    groups, scale,
    s_in, w_in, ph_in, rt_in, ct_in,
    out_r, out_c,
    S, W, PH, RT, CT, R, C, RC, RY, RZ, RS, RF, CX, CS, CR,
    local_sem, w_send, w_recv, s_send, s_recv, t_send, t_recv,
    rc_send, rc_recv, ry_send, ry_recv, rz_send, rz_recv,
    cx_send, cx_recv, cz_send, cz_recv,
):
    G = groups
    d, f = lax.axis_index("dp"), lax.axis_index("feat")
    z, x = d // 2, d % 2
    y, c = f // 2, f % 2
    fy, fc = (1 - y) * 2 + c, y * 2 + (1 - c)
    dx = z * 2 + (1 - x)
    x_peer, y_peer, c_peer = (dx, f), (d, fy), (d, fc)

    rows, width = s_in.shape
    depth = w_in.shape[0]
    cols = w_in.shape[1] // G
    rank = ct_in.shape[0]
    t_rows = rank // 4
    c_rows = rank // (2 * G)
    r_rows = rows // 4

    def zid(j):
        return (z + j) % G

    def z_peer(j):
        return (zid(j) * 2 + x, f)

    barrier = pltpu.get_barrier_semaphore()
    peers = [z_peer(j) for j in range(1, G)] + [x_peer, y_peer, c_peer]
    for peer in peers:
        pl.semaphore_signal(barrier, inc=1, device_id=peer, device_id_type=MESH)

    def w_block(who):
        return W.at[pl.ds(pl.multiple_of(who * depth, depth), depth), :]

    def s_block(zz, ff):
        return S.at[
            pl.ds(pl.multiple_of(zz * rows, rows), rows),
            pl.ds(pl.multiple_of(ff * width, LANES), width),
        ]

    def t_block(zz, ff):
        return CT.at[
            pl.ds(pl.multiple_of(ff * t_rows, t_rows), t_rows),
            pl.ds(pl.multiple_of(zz * rows, LANES), rows),
        ]

    def w_cols(zz):
        return w_in.at[:, pl.ds(pl.multiple_of(zz * cols, LANES), cols)]

    own_t = ct_in.at[pl.ds(pl.multiple_of(f * t_rows, t_rows), t_rows), :]
    col0 = pl.multiple_of(z * cols, LANES)

    locals_ = [
        pltpu.make_async_copy(w_cols(z), w_block(d), local_sem.at[0]),
        pltpu.make_async_copy(s_in, s_block(z, f), local_sem.at[1]),
        pltpu.make_async_copy(own_t, t_block(z, f), local_sem.at[2]),
        pltpu.make_async_copy(rt_in.at[pl.ds(col0, cols), :], RT, local_sem.at[3]),
        pltpu.make_async_copy(ph_in.at[:, pl.ds(col0, cols)], PH, local_sem.at[4]),
    ]
    for copy in locals_:
        copy.start()

    started = []

    def send(src, dst, ssem, rsem, peer):
        copy = pltpu.make_async_remote_copy(
            src_ref=src, dst_ref=dst, send_sem=ssem, recv_sem=rsem,
            device_id=peer, device_id_type=MESH,
        )
        copy.start()
        started.append(copy)

    def arrive(dst, ssem, rsem):
        pltpu.make_async_remote_copy(
            src_ref=dst, dst_ref=dst, send_sem=ssem, recv_sem=rsem,
            device_id=x_peer, device_id_type=MESH,
        ).wait_recv()

    counts = {"s": 0}

    def send_st(s_src, t_src, zz, ff, peer):
        n = counts["s"]
        counts["s"] = n + 1
        index = zz * 4 + ff
        send(s_src, s_block(zz, ff), s_send.at[n], s_recv.at[index], peer)
        send(t_src, t_block(zz, ff), t_send.at[n], t_recv.at[index], peer)

    def arrive_st(zz, ff):
        index = zz * 4 + ff
        arrive(s_block(zz, ff), s_send.at[0], s_recv.at[index])
        arrive(t_block(zz, ff), t_send.at[0], t_recv.at[index])

    pl.semaphore_wait(barrier, len(peers))

    for j in range(G - 1, 0, -1):
        send(w_cols(zid(j)), w_block(d), w_send.at[j], w_recv.at[d], z_peer(j))
    send(w_cols(z), w_block(d), w_send.at[0], w_recv.at[d], x_peer)
    send_st(s_in, own_t, z, f, y_peer)
    send_st(s_in, own_t, z, f, c_peer)
    for j in range(G - 1, 0, -1):
        send_st(s_in, own_t, z, f, z_peer(j))

    R[...] = jnp.zeros_like(R)
    C[...] = jnp.zeros_like(C)
    for copy in locals_:
        copy.wait()
    PH[...] = PH[...] * INV_TURN

    arrive_st(z, fy)
    send_st(s_block(z, fy), t_block(z, fy), z, fy, c_peer)
    for j in range(1, G):
        who = zid(j) * 2 + x
        arrive(w_block(who), w_send.at[0], w_recv.at[who])
        send(w_block(who), w_block(who), w_send.at[G - 1 + j], w_recv.at[who], x_peer)

    def relay_first(j):
        arrive_st(zid(j), f)
        own = (s_block(zid(j), f), t_block(zid(j), f))
        send_st(*own, zid(j), f, y_peer)
        send_st(*own, zid(j), f, c_peer)

    def relay_second(j):
        arrive_st(zid(j), fy)
        send_st(s_block(zid(j), fy), t_block(zid(j), fy), zid(j), fy, c_peer)

    tile_r, tile_c = min(512, rows), min(512, cols)
    col_tiles = cols // tile_c
    steps = (rows // tile_r) * col_tiles

    def compute(base):
        @pl.loop(0, steps)
        def _(t):
            r0 = pl.multiple_of(base + (t // col_tiles) * tile_r, tile_r)
            c0 = pl.multiple_of((t % col_tiles) * tile_c, tile_c)
            here, there = pl.ds(r0, tile_r), pl.ds(c0, tile_c)
            proj = jnp.dot(S[here, :], W[:, there], preferred_element_type=jnp.float32)
            feats = scaled_cos(proj * INV_TURN + PH[:, there], scale).astype(jnp.bfloat16)
            R[here, :] += jnp.dot(feats, RT[there, :], preferred_element_type=jnp.float32)
            C[:, there] += jnp.dot(CT[:, here], feats, preferred_element_type=jnp.float32)

    def r_part(k, yy, cc):
        start = zid(k) * rows + (yy * 2 + cc) * r_rows
        return R.at[pl.ds(pl.multiple_of(start, r_rows), r_rows), :]

    def range_core(k):
        for q, yy in enumerate((1 - y, y)):
            send(r_part(k, yy, 1 - c), RC.at[2 * k + q], rc_send.at[2 * k + q],
                 rc_recv.at[2 * k + q], c_peer)

    def range_y(k):
        arrive(RC.at[2 * k], rc_send.at[0], rc_recv.at[2 * k])
        RS[k] = r_part(k, 1 - y, c)[...] + RC[2 * k]
        send(RS.at[k], RY.at[k], ry_send.at[k], ry_recv.at[k], y_peer)

    def range_z(k):
        arrive(RC.at[2 * k + 1], rc_send.at[0], rc_recv.at[2 * k + 1])
        arrive(RY.at[k], ry_send.at[0], ry_recv.at[k])
        total = r_part(k, y, c)[...] + RC[2 * k + 1] + RY[k]
        if k == 0:
            out_r[...] = total
        else:
            RF[k] = total.astype(RF.dtype)
            send(RF.at[k], RZ.at[k], rz_send.at[k], rz_recv.at[k], z_peer(k))

    if G > 1:
        relay_first(1)
    for j in range(G):
        who = zid(j) * 2 + (1 - x)
        arrive(w_block(who), w_send.at[0], w_recv.at[who])

    for k in range(G):
        if k + 1 < G:
            relay_second(k + 1)
        if k + 2 < G:
            relay_first(k + 2)
        arrive_st(zid(k), fc)
        arrive_st(zid(k), (1 - y) * 2 + (1 - c))
        compute(zid(k) * rows)
        range_core(k)
        if k >= 1:
            range_y(k - 1)
        if k >= 2:
            range_z(k - 2)

    def c_part(j, xx):
        start = (zid(j) * 2 + xx) * c_rows
        return C.at[pl.ds(pl.multiple_of(start, c_rows), c_rows), :]

    order = list(range(1, G)) + [0]
    for j in order:
        send(c_part(j, 1 - x), CX.at[j], cx_send.at[j], cx_recv.at[j], x_peer)
    range_y(G - 1)
    if G >= 2:
        range_z(G - 2)
    for j in order:
        arrive(CX.at[j], cx_send.at[0], cx_recv.at[j])
        total = c_part(j, x)[...] + CX[j]
        if j == 0:
            out_c[:, pl.ds(col0, cols)] = total
        else:
            CS[j] = total.astype(CS.dtype)
            send(CS.at[j], CR.at[j], cz_send.at[j], cz_recv.at[j], z_peer(j))
    range_z(G - 1)

    for j in range(1, G):
        arrive(RZ.at[j], rz_send.at[0], rz_recv.at[j])
        out_r[...] += RZ[j].astype(jnp.float32)
    for j in range(1, G):
        arrive(CR.at[j], cz_send.at[0], cz_recv.at[j])
        source = pl.multiple_of(((z - j + G) % G) * cols, LANES)
        out_c[:, pl.ds(source, cols)] = CR[j].astype(jnp.float32)
    for copy in started:
        copy.wait_send()


def in_kernel(samples, freqs, phases, range_test, corange_test):
    G = lax.axis_size("dp") // 2
    rows, width = samples.shape
    depth, all_cols = freqs.shape
    cols = all_cols // G
    rank = corange_test.shape[0]
    f32, bf16 = jnp.float32, jnp.bfloat16
    scale = math.sqrt(2.0 / (all_cols * 4))
    V, DMA = pltpu.VMEM, pltpu.SemaphoreType.DMA
    block = (rows // 4, rank)
    crow = (rank // (2 * G), cols)
    any_spec = pl.BlockSpec(memory_space=pl.ANY)
    vmem_spec = pl.BlockSpec(memory_space=pltpu.VMEM)
    flops = 2 * G * rows * cols * (4 * width + 2 * rank)
    return pl.pallas_call(
        functools.partial(kernel, G, scale),
        out_shape=(
            jax.ShapeDtypeStruct(block, f32),
            jax.ShapeDtypeStruct((rank // (2 * G), all_cols), f32),
        ),
        in_specs=[any_spec] * 5,
        out_specs=(vmem_spec, vmem_spec),
        scratch_shapes=[
            V((G * rows, 4 * width), bf16),
            V((2 * G * depth, cols), bf16),
            V((1, cols), f32),
            V((cols, rank), bf16),
            V((rank, G * rows), bf16),
            V((G * rows, rank), f32),
            V((rank, cols), f32),
            V((2 * G, *block), f32),
            V((G, *block), f32),
            V((G, *block), WIRE),
            V((G, *block), f32),
            V((G, *block), WIRE),
            V((G, *crow), f32),
            V((G, *crow), WIRE),
            V((G, *crow), WIRE),
            DMA((5,)),
            DMA((2 * G,)), DMA((2 * G,)),
            DMA((4 * G,)), DMA((4 * G,)),
            DMA((4 * G,)), DMA((4 * G,)),
            DMA((2 * G,)), DMA((2 * G,)),
            DMA((G,)), DMA((G,)),
            DMA((G,)), DMA((G,)),
            DMA((G,)), DMA((G,)),
            DMA((G,)), DMA((G,)),
        ],
        compiler_params=pltpu.CompilerParams(
            collective_id=0, has_side_effects=True, vmem_limit_bytes=56 * 2**20
        ),
        cost_estimate=pl.CostEstimate(
            flops=flops, bytes_accessed=2**24, transcendentals=0
        ),
    )(samples, freqs, phases[None, :], range_test, corange_test)


def with_collectives(samples, freqs, phases, range_test, corange_test):
    scale = math.sqrt(2.0 / (freqs.shape[1] * lax.axis_size("feat")))
    projection = jnp.dot(
        lax.all_gather(samples, "feat", axis=1, tiled=True),
        lax.all_gather(freqs, "dp", axis=0, tiled=True),
        preferred_element_type=jnp.float32,
    )
    turns = projection * INV_TURN + phases[None, :] * INV_TURN
    features = scaled_cos(turns, scale).astype(jnp.bfloat16)
    range_sketch = lax.psum_scatter(
        jnp.dot(features, range_test, preferred_element_type=jnp.float32),
        "feat", scatter_dimension=0, tiled=True,
    )
    corange_sketch = lax.psum_scatter(
        jnp.dot(corange_test, features, preferred_element_type=jnp.float32),
        "dp", scatter_dimension=0, tiled=True,
    )
    return (range_sketch, corange_sketch)


def on_device(samples, freqs, phases, range_test, corange_test):
    groups = lax.axis_size("dp") // 2
    fits = (
        lax.axis_size("feat") == 4
        and lax.axis_size("dp") == 2 * groups
        and groups in (2, 4)
        and samples.shape[1] % LANES == 0
    )
    run = in_kernel if fits else with_collectives
    return run(samples, freqs, phases, range_test, corange_test)


def solution(mesh):
    placed = (P("dp", "feat"), P("dp", "feat"), P("feat"), P("feat", None), P(None, "dp"))
    return jax.shard_map(
        on_device,
        mesh=mesh,
        in_specs=placed,
        out_specs=(P(("dp", "feat"), None), P("dp", "feat")),
        check_vma=False,
    )
```

```python
import functools
import math

import jax
import jax.numpy as jnp
from jax import lax
from jax.experimental import pallas as pl
from jax.experimental.pallas import tpu as pltpu
from jax.sharding import PartitionSpec as P

MESH = pl.DeviceIdType.MESH
INV_TURN = 1.0 / (2.0 * math.pi)
SIN_TURN = (6.283164044278293, -41.33714236799647, 81.34076878818043, -70.99343236149275)
WIRE = jnp.bfloat16
LANES = 128


def scaled_cos(turns, scale):
    nearest = lax.round(turns, lax.RoundingMethod.TO_NEAREST_EVEN)
    g = 0.25 - jnp.abs(turns - nearest)
    s = g * g
    poly = jnp.float32(SIN_TURN[-1] * scale)
    for coef in SIN_TURN[-2::-1]:
        poly = poly * s + jnp.float32(coef * scale)
    return poly * g


def kernel(
    groups, scale,
    s_in, w_in, ph_in, rt_in, ct_in,
    out_r, out_c,
    S, W, PH, RT, CT, R, C, RC, RY, RZ, RS, RF, CX, CS, CR,
    local_sem, w_send, w_recv, s_send, s_recv, t_send, t_recv,
    rc_send, rc_recv, ry_send, ry_recv, rz_send, rz_recv,
    cx_send, cx_recv, cz_send, cz_recv,
):
    G = groups
    d, f = lax.axis_index("dp"), lax.axis_index("feat")
    z, x = d // 2, d % 2
    y, c = f // 2, f % 2
    fy, fc = (1 - y) * 2 + c, y * 2 + (1 - c)
    dx = z * 2 + (1 - x)
    x_peer, y_peer, c_peer = (dx, f), (d, fy), (d, fc)

    rows, width = s_in.shape
    depth = w_in.shape[0]
    cols = w_in.shape[1] // G
    rank = ct_in.shape[0]
    t_rows = rank // 4
    c_rows = rank // (2 * G)
    r_rows = rows // 4

    def zid(j):
        return (z + j) % G

    def z_peer(j):
        return (zid(j) * 2 + x, f)

    barrier = pltpu.get_barrier_semaphore()
    peers = [z_peer(j) for j in range(1, G)] + [x_peer, y_peer, c_peer]
    for peer in peers:
        pl.semaphore_signal(barrier, inc=1, device_id=peer, device_id_type=MESH)

    def w_block(who):
        return W.at[pl.ds(pl.multiple_of(who * depth, depth), depth), :]

    def s_block(zz, ff):
        return S.at[
            pl.ds(pl.multiple_of(zz * rows, rows), rows),
            pl.ds(pl.multiple_of(ff * width, LANES), width),
        ]

    def t_block(zz, ff):
        return CT.at[
            pl.ds(pl.multiple_of(ff * t_rows, t_rows), t_rows),
            pl.ds(pl.multiple_of(zz * rows, LANES), rows),
        ]

    def w_cols(zz):
        return w_in.at[:, pl.ds(pl.multiple_of(zz * cols, LANES), cols)]

    own_t = ct_in.at[pl.ds(pl.multiple_of(f * t_rows, t_rows), t_rows), :]
    col0 = pl.multiple_of(z * cols, LANES)

    locals_ = [
        pltpu.make_async_copy(w_cols(z), w_block(d), local_sem.at[0]),
        pltpu.make_async_copy(s_in, s_block(z, f), local_sem.at[1]),
        pltpu.make_async_copy(own_t, t_block(z, f), local_sem.at[2]),
        pltpu.make_async_copy(rt_in.at[pl.ds(col0, cols), :], RT, local_sem.at[3]),
        pltpu.make_async_copy(ph_in.at[:, pl.ds(col0, cols)], PH, local_sem.at[4]),
    ]
    for copy in locals_:
        copy.start()

    started = []

    def send(src, dst, ssem, rsem, peer):
        copy = pltpu.make_async_remote_copy(
            src_ref=src, dst_ref=dst, send_sem=ssem, recv_sem=rsem,
            device_id=peer, device_id_type=MESH,
        )
        copy.start()
        started.append(copy)

    def arrive(dst, ssem, rsem):
        pltpu.make_async_remote_copy(
            src_ref=dst, dst_ref=dst, send_sem=ssem, recv_sem=rsem,
            device_id=x_peer, device_id_type=MESH,
        ).wait_recv()

    counts = {"s": 0}

    def send_st(s_src, t_src, zz, ff, peer):
        n = counts["s"]
        counts["s"] = n + 1
        index = zz * 4 + ff
        send(s_src, s_block(zz, ff), s_send.at[n], s_recv.at[index], peer)
        send(t_src, t_block(zz, ff), t_send.at[n], t_recv.at[index], peer)

    def arrive_st(zz, ff):
        index = zz * 4 + ff
        arrive(s_block(zz, ff), s_send.at[0], s_recv.at[index])
        arrive(t_block(zz, ff), t_send.at[0], t_recv.at[index])

    pl.semaphore_wait(barrier, len(peers))

    for j in range(G - 1, 0, -1):
        send(w_cols(zid(j)), w_block(d), w_send.at[j], w_recv.at[d], z_peer(j))
    send(w_cols(z), w_block(d), w_send.at[0], w_recv.at[d], x_peer)
    send_st(s_in, own_t, z, f, y_peer)
    send_st(s_in, own_t, z, f, c_peer)
    for j in range(G - 1, 0, -1):
        send_st(s_in, own_t, z, f, z_peer(j))

    R[...] = jnp.zeros_like(R)
    C[...] = jnp.zeros_like(C)
    for copy in locals_:
        copy.wait()
    PH[...] = PH[...] * INV_TURN

    arrive_st(z, fy)
    send_st(s_block(z, fy), t_block(z, fy), z, fy, c_peer)
    for j in range(1, G):
        who = zid(j) * 2 + x
        arrive(w_block(who), w_send.at[0], w_recv.at[who])
        send(w_block(who), w_block(who), w_send.at[G - 1 + j], w_recv.at[who], x_peer)

    def relay_first(j):
        arrive_st(zid(j), f)
        own = (s_block(zid(j), f), t_block(zid(j), f))
        send_st(*own, zid(j), f, y_peer)
        send_st(*own, zid(j), f, c_peer)

    def relay_second(j):
        arrive_st(zid(j), fy)
        send_st(s_block(zid(j), fy), t_block(zid(j), fy), zid(j), fy, c_peer)

    tile_r, tile_c = min(512, rows), min(512, cols)
    col_tiles = cols // tile_c
    steps = (rows // tile_r) * col_tiles

    def compute(base):
        @pl.loop(0, steps)
        def _(t):
            r0 = pl.multiple_of(base + (t // col_tiles) * tile_r, tile_r)
            c0 = pl.multiple_of((t % col_tiles) * tile_c, tile_c)
            here, there = pl.ds(r0, tile_r), pl.ds(c0, tile_c)
            proj = jnp.dot(S[here, :], W[:, there], preferred_element_type=jnp.float32)
            feats = scaled_cos(proj * INV_TURN + PH[:, there], scale).astype(jnp.bfloat16)
            R[here, :] += jnp.dot(feats, RT[there, :], preferred_element_type=jnp.float32)
            C[:, there] += jnp.dot(CT[:, here], feats, preferred_element_type=jnp.float32)

    def r_part(k, yy, cc):
        start = zid(k) * rows + (yy * 2 + cc) * r_rows
        return R.at[pl.ds(pl.multiple_of(start, r_rows), r_rows), :]

    def range_core(k):
        for q, yy in enumerate((1 - y, y)):
            send(r_part(k, yy, 1 - c), RC.at[2 * k + q], rc_send.at[2 * k + q],
                 rc_recv.at[2 * k + q], c_peer)

    def range_y(k):
        arrive(RC.at[2 * k], rc_send.at[0], rc_recv.at[2 * k])
        RS[k] = r_part(k, 1 - y, c)[...] + RC[2 * k]
        send(RS.at[k], RY.at[k], ry_send.at[k], ry_recv.at[k], y_peer)

    def range_z(k):
        arrive(RC.at[2 * k + 1], rc_send.at[0], rc_recv.at[2 * k + 1])
        arrive(RY.at[k], ry_send.at[0], ry_recv.at[k])
        total = r_part(k, y, c)[...] + RC[2 * k + 1] + RY[k]
        if k == 0:
            out_r[...] = total
        else:
            RF[k] = total.astype(RF.dtype)
            send(RF.at[k], RZ.at[k], rz_send.at[k], rz_recv.at[k], z_peer(k))

    if G > 1:
        relay_first(1)
    for j in range(G):
        who = zid(j) * 2 + (1 - x)
        arrive(w_block(who), w_send.at[0], w_recv.at[who])

    for k in range(G):
        if k + 1 < G:
            relay_second(k + 1)
        if k + 2 < G:
            relay_first(k + 2)
        arrive_st(zid(k), fc)
        arrive_st(zid(k), (1 - y) * 2 + (1 - c))
        compute(zid(k) * rows)
        range_core(k)
        if k >= 1:
            range_y(k - 1)
        if k >= 2:
            range_z(k - 2)

    def c_part(j, xx):
        start = (zid(j) * 2 + xx) * c_rows
        return C.at[pl.ds(pl.multiple_of(start, c_rows), c_rows), :]

    order = list(range(1, G)) + [0]
    for j in order:
        send(c_part(j, 1 - x), CX.at[j], cx_send.at[j], cx_recv.at[j], x_peer)
    range_y(G - 1)
    if G >= 2:
        range_z(G - 2)
    for j in order:
        arrive(CX.at[j], cx_send.at[0], cx_recv.at[j])
        total = c_part(j, x)[...] + CX[j]
        if j == 0:
            out_c[:, pl.ds(col0, cols)] = total
        else:
            CS[j] = total.astype(CS.dtype)
            send(CS.at[j], CR.at[j], cz_send.at[j], cz_recv.at[j], z_peer(j))
    range_z(G - 1)

    for j in range(1, G):
        arrive(RZ.at[j], rz_send.at[0], rz_recv.at[j])
        out_r[...] += RZ[j].astype(jnp.float32)
    for j in range(1, G):
        arrive(CR.at[j], cz_send.at[0], cz_recv.at[j])
        source = pl.multiple_of(((z - j + G) % G) * cols, LANES)
        out_c[:, pl.ds(source, cols)] = CR[j].astype(jnp.float32)
    for copy in started:
        copy.wait_send()


def in_kernel(samples, freqs, phases, range_test, corange_test):
    G = lax.axis_size("dp") // 2
    rows, width = samples.shape
    depth, all_cols = freqs.shape
    cols = all_cols // G
    rank = corange_test.shape[0]
    f32, bf16 = jnp.float32, jnp.bfloat16
    scale = math.sqrt(2.0 / (all_cols * 4))
    V, DMA = pltpu.VMEM, pltpu.SemaphoreType.DMA
    block = (rows // 4, rank)
    crow = (rank // (2 * G), cols)
    any_spec = pl.BlockSpec(memory_space=pl.ANY)
    vmem_spec = pl.BlockSpec(memory_space=pltpu.VMEM)
    flops = 2 * G * rows * cols * (4 * width + 2 * rank)
    return pl.pallas_call(
        functools.partial(kernel, G, scale),
        out_shape=(
            jax.ShapeDtypeStruct(block, f32),
            jax.ShapeDtypeStruct((rank // (2 * G), all_cols), f32),
        ),
        in_specs=[any_spec] * 5,
        out_specs=(vmem_spec, vmem_spec),
        scratch_shapes=[
            V((G * rows, 4 * width), bf16),
            V((2 * G * depth, cols), bf16),
            V((1, cols), f32),
            V((cols, rank), bf16),
            V((rank, G * rows), bf16),
            V((G * rows, rank), f32),
            V((rank, cols), f32),
            V((2 * G, *block), f32),
            V((G, *block), f32),
            V((G, *block), WIRE),
            V((G, *block), f32),
            V((G, *block), WIRE),
            V((G, *crow), f32),
            V((G, *crow), WIRE),
            V((G, *crow), WIRE),
            DMA((5,)),
            DMA((2 * G,)), DMA((2 * G,)),
            DMA((4 * G,)), DMA((4 * G,)),
            DMA((4 * G,)), DMA((4 * G,)),
            DMA((2 * G,)), DMA((2 * G,)),
            DMA((G,)), DMA((G,)),
            DMA((G,)), DMA((G,)),
            DMA((G,)), DMA((G,)),
            DMA((G,)), DMA((G,)),
        ],
        compiler_params=pltpu.CompilerParams(
            collective_id=0, has_side_effects=True, vmem_limit_bytes=56 * 2**20
        ),
        cost_estimate=pl.CostEstimate(
            flops=flops, bytes_accessed=2**24, transcendentals=0
        ),
    )(samples, freqs, phases[None, :], range_test, corange_test)


def with_collectives(samples, freqs, phases, range_test, corange_test):
    scale = math.sqrt(2.0 / (freqs.shape[1] * lax.axis_size("feat")))
    projection = jnp.dot(
        lax.all_gather(samples, "feat", axis=1, tiled=True),
        lax.all_gather(freqs, "dp", axis=0, tiled=True),
        preferred_element_type=jnp.float32,
    )
    turns = projection * INV_TURN + phases[None, :] * INV_TURN
    features = scaled_cos(turns, scale).astype(jnp.bfloat16)
    range_sketch = lax.psum_scatter(
        jnp.dot(features, range_test, preferred_element_type=jnp.float32),
        "feat", scatter_dimension=0, tiled=True,
    )
    corange_sketch = lax.psum_scatter(
        jnp.dot(corange_test, features, preferred_element_type=jnp.float32),
        "dp", scatter_dimension=0, tiled=True,
    )
    return (range_sketch, corange_sketch)


def on_device(samples, freqs, phases, range_test, corange_test):
    groups = lax.axis_size("dp") // 2
    fits = (
        lax.axis_size("feat") == 4
        and lax.axis_size("dp") == 2 * groups
        and groups in (2, 4)
        and samples.shape[1] % LANES == 0
    )
    run = in_kernel if fits else with_collectives
    return run(samples, freqs, phases, range_test, corange_test)


def solution(mesh):
    placed = (P("dp", "feat"), P("dp", "feat"), P("feat"), P("feat", None), P(None, "dp"))
    return jax.shard_map(
        on_device,
        mesh=mesh,
        in_specs=placed,
        out_specs=(P(("dp", "feat"), None), P("dp", "feat")),
        check_vma=False,
    )
```
